256 devices in a mesh: ctx: 64 (over x_hi, z, y), head: 4 (over x_lo, core).
Axes of the slice: x: 4 (x_hi: 2, x_lo: 2; x = x_hi * 2 + x_lo), y: 4, z: 8, core: 2. Of those that a mesh axis runs over, the one named last changes fastest.
Arguments:
- queries: bfloat16 [32768, 3072], P(('ctx', 'head')), may hold values from -6 to 6
- keys: bfloat16 [32768, 3072], P(('ctx', 'head')), may hold values from -6 to 6
- values: bfloat16 [32768, 3072], P(('ctx', 'head')), may hold values from -6 to 6
- outputs: bfloat16 [32768, 3072], P(('ctx', 'head')), may hold values from -4 to 4
- out_grads: bfloat16 [32768, 3072], P(('ctx', 'head')), may hold values from -6 to 6
- log_sums: float32 [32768, 24], P(('ctx', 'head')), may hold values from 2.5 to 4.5
- window_mask: int32 [128, 5], replicated, may hold values 0 or 1
- context_flag: int32 [128], replicated, may hold values 0 or 1
Outputs:
- query_grads: bfloat16 [32768, 3072], P(('ctx', 'head'))
- key_grads: bfloat16 [32768, 3072], P(('ctx', 'head'))
- value_grads: bfloat16 [32768, 3072], P(('ctx', 'head'))
The draws below stay inside these ranges and needn't reach their ends.
All inputs are finite; a program needn't handle non-finite values.
Results may differ from the reference program's by a relative error of at most 0.0046.
The reference program's roundings to bfloat16 on the way (of `probs_b` and `dscores_b`) count: a program that leaves them out, or rounds other values in their place, can miss the bound.
Values may be sent and summed in bfloat16 or wider, within the bound.
A program may use at most 128 MiB of HBM per device.

```python
import jax
import jax.numpy as jnp
from jax import lax

HEADS = 24
HD = 128
TILE_TOKENS = 256
WIN = 2
TOKENS = 32768
TILE_COUNT = 128


def set_ends(drawn, own_key, low, top_value):
    dims = drawn.shape
    place = [jax.random.randint(jax.random.fold_in(own_key, axis), (), 0, dims[axis]) for axis in range(len(dims))]
    drawn = drawn.at[tuple(place)].set(low)
    longest = dims.index(max(dims))
    place[longest] = (place[longest] + 1) % dims[longest]
    return drawn.at[tuple(place)].set(top_value)


def block_levels(rng, extent, cuts, smallest, largest):
    def one(dim, parts):
        steps = jax.random.uniform(jax.random.fold_in(jax.random.fold_in(rng, 6), dim), (parts,), jnp.float32, smallest / len(cuts), largest / len(cuts))
        return jnp.repeat(jnp.exp(steps), extent[dim] // parts).reshape((-1,) + (1,) * (len(extent) - dim - 1))

    loudness = one(*cuts[0])
    for cut in cuts[1:]:
        loudness = loudness * one(*cut)
    return loudness


def bell_draw(own_key, dims, scale, most, pieces=(), kind=jnp.bfloat16):
    gain = block_levels(own_key, dims, pieces, -0.22, 0.18) if pieces else 1.0
    values = jax.random.normal(own_key, dims, jnp.float32) * scale * gain
    return jnp.minimum(jnp.maximum(values, -most), most).astype(kind)


def setup_inputs(seed: int = 0) -> dict:
    splits = jax.random.split(jax.random.key(seed), 9)
    return {
        "queries": bell_draw(splits[0], (TOKENS, HEADS * HD), 1.0, 6.0, ((0, 256),)),
        "keys": bell_draw(splits[1], (TOKENS, HEADS * HD), 1.0, 6.0, ((0, 256),)),
        "values": bell_draw(splits[2], (TOKENS, HEADS * HD), 1.0, 6.0, ((0, 256),)),
        "outputs": bell_draw(splits[3], (TOKENS, HEADS * HD), 0.5, 4.0, ((0, 256),)),
        "out_grads": bell_draw(splits[4], (TOKENS, HEADS * HD), 1.0, 6.0, ((0, 256),)),
        "log_sums": jnp.clip(2.5 + 2.0 * jax.random.uniform(splits[5], (TOKENS, HEADS), jnp.float32) ** block_levels(splits[5], (TOKENS, HEADS), ((0, 256),), -0.2, 0.2), 2.5, 4.5),
        "window_mask": set_ends((jax.random.randint(splits[6], (TILE_COUNT, 2 * WIN + 1), 0, 4) < 3).astype(jnp.int32), jax.random.fold_in(splits[6], 1), 0, 1),
        "context_flag": set_ends((jax.random.randint(splits[7], (TILE_COUNT,), 0, 4) < 1).astype(jnp.int32), jax.random.fold_in(splits[7], 1), 0, 1),
    }


def tile_allowed(query_tiles, key_tiles, window_mask, context_flag, total_tiles, reach):
    offset = (key_tiles[None, :] - query_tiles[:, None] + reach) % total_tiles
    inside = offset <= 2 * reach
    column = jnp.minimum(offset, 2 * reach).astype(jnp.int32)
    table = window_mask[query_tiles]
    picked = jnp.take_along_axis(table, column, axis=1)
    window_ok = (picked == 1) | (offset == reach)
    ctx_query = context_flag[query_tiles][:, None]
    ctx_key = context_flag[key_tiles][None, :]
    return inside & window_ok & ((ctx_query == 0) | (ctx_key == 1))


def expand_mask(allowed, tile):
    count_q, count_k = allowed.shape
    full = jnp.broadcast_to(allowed[:, None, :, None], (count_q, tile, count_k, tile))
    return full.reshape(count_q * tile, count_k * tile)


def block_grads(q_blk, do_blk, lse_blk, delta_blk, k_blk, v_blk, mask, scale):
    qf = q_blk.astype(jnp.float32)
    dof = do_blk.astype(jnp.float32)
    kf = k_blk.astype(jnp.float32)
    vf = v_blk.astype(jnp.float32)
    scores = jnp.einsum("qhd,khd->hqk", qf, kf) * scale
    probs = jnp.where(mask[None], jnp.exp(scores - lse_blk.T[:, :, None]), jnp.float32(0.0))
    dprobs = jnp.einsum("qhd,khd->hqk", dof, vf)
    dscores = probs * (dprobs - delta_blk.T[:, :, None])
    probs_b = probs.astype(jnp.bfloat16).astype(jnp.float32)
    dscores_b = dscores.astype(jnp.bfloat16).astype(jnp.float32)
    value_gradient = jnp.einsum("hqk,qhd->khd", probs_b, dof)
    grad_k = jnp.einsum("hqk,qhd->khd", dscores_b, qf) * scale
    query_gradient = jnp.einsum("hqk,khd->qhd", dscores_b, kf) * scale
    return query_gradient, grad_k, value_gradient


def reference(queries, keys, values, outputs, out_grads, log_sums, window_mask, context_flag):
    scale = HD ** -0.5
    tile_span = 2 * WIN + 1
    border_tiles = WIN * TILE_TOKENS
    q3 = queries.reshape(TOKENS, HEADS, HD)
    k3 = keys.reshape(TOKENS, HEADS, HD)
    v3 = values.reshape(TOKENS, HEADS, HD)
    do3 = out_grads.reshape(TOKENS, HEADS, HD)
    o3 = outputs.reshape(TOKENS, HEADS, HD)
    delta = jnp.sum(do3.astype(jnp.float32) * o3.astype(jnp.float32), axis=2)
    key_ext = jnp.concatenate([k3[TOKENS - border_tiles:], k3, k3[:border_tiles]], axis=0)
    val_ext = jnp.concatenate([v3[TOKENS - border_tiles:], v3, v3[:border_tiles]], axis=0)
    offsets = jnp.arange(tile_span, dtype=jnp.int32)

    def loop_step(s, loop_carry):
        query_gradient, grad_k, value_gradient = loop_carry
        start_index = (s * TILE_TOKENS).astype(jnp.int32)
        q_blk = lax.dynamic_slice_in_dim(q3, start_index, TILE_TOKENS, 0)
        do_blk = lax.dynamic_slice_in_dim(do3, start_index, TILE_TOKENS, 0)
        lse_blk = lax.dynamic_slice_in_dim(log_sums, start_index, TILE_TOKENS, 0)
        delta_blk = lax.dynamic_slice_in_dim(delta, start_index, TILE_TOKENS, 0)
        k_blk = lax.dynamic_slice_in_dim(key_ext, start_index, tile_span * TILE_TOKENS, 0)
        v_blk = lax.dynamic_slice_in_dim(val_ext, start_index, tile_span * TILE_TOKENS, 0)
        query_tiles = jnp.reshape(s, (1,)).astype(jnp.int32)
        key_tiles = ((s - WIN + offsets) % TILE_COUNT).astype(jnp.int32)
        allowed = tile_allowed(query_tiles, key_tiles, window_mask, context_flag, TILE_COUNT, WIN)
        mask = expand_mask(allowed, TILE_TOKENS)
        gq, gk, value_grad_block = block_grads(q_blk, do_blk, lse_blk, delta_blk, k_blk, v_blk, mask, scale)
        query_gradient = lax.dynamic_update_slice_in_dim(query_gradient, gq, start_index, 0)
        old_k = lax.dynamic_slice_in_dim(grad_k, start_index, tile_span * TILE_TOKENS, 0)
        previous_value = lax.dynamic_slice_in_dim(value_gradient, start_index, tile_span * TILE_TOKENS, 0)
        grad_k = lax.dynamic_update_slice_in_dim(grad_k, old_k + gk, start_index, 0)
        value_gradient = lax.dynamic_update_slice_in_dim(value_gradient, previous_value + value_grad_block, start_index, 0)
        return query_gradient, grad_k, value_gradient

    query_zeros = jnp.zeros((TOKENS, HEADS, HD), jnp.float32)
    extended_zeros = jnp.zeros((TOKENS + 2 * border_tiles, HEADS, HD), jnp.float32)
    query_gradient, key_extended, value_extended = lax.fori_loop(0, TILE_COUNT, loop_step, (query_zeros, extended_zeros, extended_zeros))

    def fold_tiles(ext):
        inner = ext[border_tiles:border_tiles + TOKENS]
        inner = inner.at[TOKENS - border_tiles:].add(ext[:border_tiles])
        inner = inner.at[:border_tiles].add(ext[border_tiles + TOKENS:])
        return inner

    grad_k = fold_tiles(key_extended)
    value_gradient = fold_tiles(value_extended)
    shape = (TOKENS, HEADS * HD)
    return (query_gradient.reshape(shape).astype(jnp.bfloat16), grad_k.reshape(shape).astype(jnp.bfloat16), value_gradient.reshape(shape).astype(jnp.bfloat16))
```

```python
import functools

import jax
import jax.numpy as jnp
from jax import lax
from jax.experimental import pallas as pl
from jax.experimental.pallas import tpu as pltpu
from jax.sharding import PartitionSpec as P

TILE = 256
HD = 128
WIN = 2
AHEAD = 2
LOG2E = 1.4426950408889634
OFF = 1e30
MESH = pl.DeviceIdType.MESH
NT = (((1,), (1,)), ((), ()))


def matmul(a, b):
    return jnp.dot(a, b, preferred_element_type=jnp.float32)


def kernel(
    ctx_count,
    heads,
    q_ref, k_ref, v_ref, o_ref, do_ref, lse_ref, wm_ref, cf_ref,
    dq_ref, dk_ref, dv_ref,
    own, halo, stat_send, stat, stat_halo, o_buf, do_buf, rows,
    acc_kv, acc_q, part_send, part, out,
    s_load, s_in, r_q, r_kv, s_stat, r_stat, s_hstat, r_hstat, s_halo, r_halo,
    s_part, r_part, s_out, r_out,
):
    tokens = q_ref.shape[0]
    groups = 4
    me_c, me_j = lax.axis_index("ctx"), lax.axis_index("head")
    half = ctx_count // 2
    flip = me_c // half
    group = lax.rem(me_j + 2 * flip, groups)
    sides = []
    for step in (ctx_count - 1, 1):
        c = lax.rem(me_c + step, ctx_count)
        sides.append((c, lax.rem(me_j + 2 * flip + 2 * (c // half), groups)))
    peers = [(r, lax.rem(me_j + r, groups), lax.rem(group + r, groups)) for r in (2, 1, 3)]
    my_rows = pl.ds(pl.multiple_of(me_j * tokens, tokens), tokens)

    def columns(which_group, head):
        return pl.ds(pl.multiple_of((which_group * heads + head) * HD, HD), HD)

    def remote(src, dst, send, recv, device):
        pltpu.make_async_remote_copy(
            src_ref=src, dst_ref=dst, send_sem=send, recv_sem=recv,
            device_id=device, device_id_type=MESH,
        ).start()

    def wait_bytes(ref, sem):
        pltpu.make_async_copy(ref, ref, sem).wait()

    load_o = pltpu.make_async_copy(o_ref, o_buf, s_load.at[0])
    load_do = pltpu.make_async_copy(do_ref, do_buf, s_load.at[1])
    load_o.start()
    load_do.start()

    barrier = pltpu.get_barrier_semaphore()
    for _, peer, _ in peers:
        pl.semaphore_signal(barrier, inc=1, device_id=(me_c, peer), device_id_type=MESH)
    for side in sides:
        pl.semaphore_signal(barrier, inc=1, device_id=side, device_id_type=MESH)
    pl.semaphore_wait(barrier, len(peers) + len(sides))

    def send_in(head):
        for first, refs, sem in ((0, (q_ref, do_ref), r_q), (2, (k_ref, v_ref), r_kv)):
            for index, ref in enumerate(refs):
                for _, peer, peer_group in peers:
                    remote(
                        ref.at[:, columns(peer_group, head)],
                        own.at[head, first + index, my_rows],
                        s_in.at[head], sem.at[head], (me_c, peer),
                    )
                pltpu.make_async_copy(
                    ref.at[:, columns(group, head)],
                    own.at[head, first + index, my_rows],
                    sem.at[head],
                ).start()

    for head in range(AHEAD):
        send_in(head)

    load_o.wait()
    load_do.wait()
    all_heads = groups * heads
    lane = lax.broadcasted_iota(jnp.int32, (tokens, HD), 1)
    columns_f = jnp.zeros((tokens, HD), jnp.float32)
    for n in range(all_heads):
        span = slice(n * HD, (n + 1) * HD)
        product = do_buf[:, span].astype(jnp.float32) * o_buf[:, span].astype(jnp.float32)
        columns_f = jnp.where(lane == 32 + n, jnp.sum(product, axis=1, keepdims=True), columns_f)
    rows[...] = columns_f
    rows[:, 0:all_heads] = lse_ref[...] * LOG2E
    turned = rows[...].T
    for g in range(groups):
        stat_send[g] = jnp.zeros((16, tokens), jnp.float32)
        stat_send[g, 0:heads] = turned[g * heads:(g + 1) * heads]
        stat_send[g, 8:8 + heads] = turned[32 + g * heads:32 + (g + 1) * heads]
    stat[me_j] = stat_send[group]
    for _, peer, peer_group in peers:
        remote(stat_send.at[peer_group], stat.at[me_j], s_stat, r_stat, (me_c, peer))

    tiles = 2 * ctx_count

    def tile_at(shift):
        return lax.rem(2 * me_c + shift + tiles, tiles)

    def off_amount(shift_q, shift_k):
        e = shift_k - shift_q + WIN
        s, u = tile_at(shift_q), tile_at(shift_k)
        open_ctx = (cf_ref[s] == 0) | (cf_ref[u] == 1)
        ok = open_ctx if e == WIN else open_ctx & (wm_ref[s, e] == 1)
        return jnp.where(ok, jnp.float32(0.0), jnp.float32(OFF))

    off = {
        (s, u): off_amount(s, u) for s in range(-2, 4) for u in (0, 1) if abs(s - u) <= WIN
    }

    scale = HD ** -0.5

    def stat_row(ref_at, tile, row):
        return jnp.concatenate(
            [ref_at(2 * tile, row), ref_at(2 * tile + 1, row)], axis=1
        )

    def pair(k, v, kt, q, do, lse, delta):
        probs = jnp.exp2(
            lax.dot_general(k, q, NT, preferred_element_type=jnp.float32) * (scale * LOG2E) - lse
        )
        dprobs = lax.dot_general(v, do, NT, preferred_element_type=jnp.float32)
        dscores = (probs * (dprobs - delta)).astype(jnp.bfloat16)
        return (
            matmul(dscores, q),
            matmul(probs.astype(jnp.bfloat16), do),
            matmul(kt, dscores),
        )

    def load_keys(head):
        made = []
        for t in range(2):
            span = pl.ds(t * TILE, TILE)
            k = own[head, 2, span]
            made.append((k, own[head, 3, span], k.T))
        return made

    def own_pairs(head):
        keys = load_keys(head)
        for s in range(2):
            span = pl.ds(s * TILE, TILE)
            q, do = own[head, 0, span], own[head, 1, span]
            row = lambda b, r: stat[b, pl.ds(r, 1)]
            lse, delta = stat_row(row, s, head), stat_row(row, s, head + 8)
            dq = None
            for t in range(2):
                dk, dv, term = pair(*keys[t], q, do, lse + off[s, t], delta)
                if s == 0:
                    acc_kv[0, t], acc_kv[1, t] = dk, dv
                else:
                    acc_kv[0, t] += dk
                    acc_kv[1, t] += dv
                dq = term if dq is None else dq + term
            acc_q[head, s] = dq

    def halo_pairs(head):
        keys = load_keys(head)
        for side in range(2):
            for s in range(2):
                shift = s - 2 if side == 0 else s + 2
                span = pl.ds(s * TILE, TILE)
                q, do = halo[head, side, 0, span], halo[head, side, 1, span]
                row = lambda b, r: stat_halo[side, b, pl.ds(r, 1)]
                lse, delta = stat_row(row, s, head), stat_row(row, s, head + 8)
                dq = None
                for t in range(2):
                    if (shift, t) not in off:
                        continue
                    dk, dv, term = pair(*keys[t], q, do, lse + off[shift, t], delta)
                    acc_kv[0, t] += dk
                    acc_kv[1, t] += dv
                    dq = term if dq is None else dq + term
                part_send[head, side, s] = (dq * scale).astype(jnp.bfloat16)
            remote(
                part_send.at[head, side], part.at[head, 1 - side],
                s_part.at[head], r_part.at[head], sides[side],
            )
        for t in range(2):
            span = pl.ds(t * TILE, TILE)
            out[head, 1, span] = (acc_kv[0, t] * scale).astype(jnp.bfloat16)
            out[head, 2, span] = acc_kv[1, t].astype(jnp.bfloat16)

    outputs = (dq_ref, dk_ref, dv_ref)

    def send_out(head, which):
        for index in which:
            target = outputs[index].at[:, columns(group, head)]
            for _, peer, _ in peers:
                rows_there = pl.ds(pl.multiple_of(peer * tokens, tokens), tokens)
                remote(
                    out.at[head, index, rows_there], target,
                    s_out.at[head], r_out.at[index], (me_c, peer),
                )
            pltpu.make_async_copy(out.at[head, index, my_rows], target, r_out.at[index]).start()

    def finish_q(head):
        for s in range(2):
            total = acc_q[head, s] * scale
            total = total + part[head, 0, s].astype(jnp.float32)
            total = total + part[head, 1, s].astype(jnp.float32)
            out[head, 0, pl.ds(s * TILE, TILE)] = total.T.astype(jnp.bfloat16)

    wait_bytes(stat.at[0:3], r_stat)
    for side in range(2):
        remote(stat, stat_halo.at[1 - side], s_hstat, r_hstat.at[1 - side], sides[side])

    def step(i, carry):
        @pl.when(i + AHEAD < heads)
        def _():
            send_in(i + AHEAD)

        @pl.when(i < heads)
        def _():
            wait_bytes(own.at[i, 0:2], r_q.at[i])
            for side in range(2):
                remote(
                    own.at[i, 0:2], halo.at[i, 1 - side],
                    s_halo.at[i], r_halo.at[i, 1 - side], sides[side],
                )

        @pl.when((i >= 1) & (i <= heads))
        def _():
            head = i - 1
            wait_bytes(own.at[head, 2:4], r_kv.at[head])
            own_pairs(head)
            for side in range(2):
                wait_bytes(halo.at[head, side], r_halo.at[head, side])
            halo_pairs(head)
            send_out(head, (1, 2))

        @pl.when(i >= 2)
        def _():
            head = i - 2
            wait_bytes(part.at[head], r_part.at[head])
            finish_q(head)
            send_out(head, (0,))

        return carry

    for side in range(2):
        wait_bytes(stat_halo.at[side], r_hstat.at[side])
    lax.fori_loop(0, heads + 2, step, 0)

    wait_bytes(stat.at[0:3], s_stat)
    wait_bytes(stat_halo, s_hstat)

    def drain(head, carry):
        wait_bytes(own.at[head, :, pl.ds(0, 3 * tokens)], s_in.at[head])
        wait_bytes(own.at[head], s_halo.at[head])
        wait_bytes(part_send.at[head], s_part.at[head])
        wait_bytes(out.at[head, :, pl.ds(0, 3 * tokens)], s_out.at[head])
        return carry

    lax.fori_loop(0, heads, drain, 0)
    for index in range(3):
        wait_bytes(outputs[index], r_out.at[index])


def per_device(queries, keys, values, outputs, out_grads, log_sums, window_mask, context_flag):
    tokens, width = queries.shape
    ctx_count, groups = lax.axis_size("ctx"), lax.axis_size("head")
    heads = log_sums.shape[1] // groups
    block = groups * tokens
    bf16, f32 = jnp.bfloat16, jnp.float32
    dma, vmem = pltpu.SemaphoreType.DMA, pltpu.VMEM
    anywhere = pl.BlockSpec(memory_space=pl.ANY)
    scalars = pl.BlockSpec(memory_space=pltpu.SMEM)
    return pl.pallas_call(
        functools.partial(kernel, ctx_count, heads),
        out_shape=[jax.ShapeDtypeStruct((tokens, width), bf16)] * 3,
        in_specs=[anywhere] * 5 + [pl.BlockSpec(memory_space=pltpu.VMEM), scalars, scalars],
        out_specs=[anywhere] * 3,
        scratch_shapes=[
            vmem((heads, 4, block, HD), bf16),
            vmem((heads, 2, 2, block, HD), bf16),
            vmem((groups, 16, tokens), f32),
            vmem((groups, 16, tokens), f32),
            vmem((2, groups, 16, tokens), f32),
            vmem((tokens, width), bf16),
            vmem((tokens, width), bf16),
            vmem((tokens, HD), f32),
            vmem((2, 2, TILE, HD), f32),
            vmem((heads, 2, HD, TILE), f32),
            vmem((heads, 2, 2, HD, TILE), bf16),
            vmem((heads, 2, 2, HD, TILE), bf16),
            vmem((heads, 3, block, HD), bf16),
            dma((2,)),
            dma((heads,)),
            dma((heads,)),
            dma((heads,)),
            dma,
            dma,
            dma,
            dma((2,)),
            dma((heads,)),
            dma((heads, 2)),
            dma((heads,)),
            dma((heads,)),
            dma((heads,)),
            dma((3,)),
        ],
        compiler_params=pltpu.CompilerParams(
            collective_id=0, has_side_effects=True, vmem_limit_bytes=40 * 1024 * 1024
        ),
        name="attention_grads",
    )(queries, keys, values, outputs, out_grads, log_sums, window_mask, context_flag)


def solution(mesh):
    placed = (P(("ctx", "head"), None),) * 6 + (P(), P())
    return jax.shard_map(
        per_device,
        mesh=mesh,
        in_specs=placed,
        out_specs=(P(("ctx", "head"), None),) * 3,
        check_vma=False,
    )
```

```python
import functools

import jax
import jax.numpy as jnp
from jax import lax
from jax.experimental import pallas as pl
from jax.experimental.pallas import tpu as pltpu
from jax.sharding import PartitionSpec as P

TILE = 256
HD = 128
WIN = 2
LOG2E = 1.4426950408889634
OFF = 1e30
MESH = pl.DeviceIdType.MESH
NT = (((1,), (1,)), ((), ()))


def matmul(a, b):
    return jnp.dot(a, b, preferred_element_type=jnp.float32)


def kernel(
    ctx_count,
    heads,
    q_ref, k_ref, v_ref, o_ref, do_ref, lse_hbm, wm_hbm, cf_hbm,
    dq_ref, dk_ref, dv_ref,
    own, halo, stat_send, stat, stat_halo, o_buf, do_buf, lse_ref, wm_ref, cf_ref, rows,
    acc_kv, acc_q, part_send, part, out,
    s_load, s_in, r_q, r_kv, s_stat, r_stat, s_hstat, r_hstat, s_halo, r_halo,
    s_part, r_part, s_out, r_out,
):
    tokens = q_ref.shape[0]
    groups = 4
    me_c, me_j = lax.axis_index("ctx"), lax.axis_index("head")
    half = ctx_count // 2
    flip = me_c // half
    group = lax.rem(me_j + 2 * flip, groups)
    sides = []
    for step in (ctx_count - 1, 1):
        c = lax.rem(me_c + step, ctx_count)
        sides.append((c, lax.rem(me_j + 2 * flip + 2 * (c // half), groups)))
    peers = [(r, lax.rem(me_j + r, groups), lax.rem(group + r, groups)) for r in (2, 1, 3)]
    my_rows = pl.ds(pl.multiple_of(me_j * tokens, tokens), tokens)

    def columns(which_group, head):
        return pl.ds(pl.multiple_of((which_group * heads + head) * HD, HD), HD)

    def remote(src, dst, send, recv, device):
        pltpu.make_async_remote_copy(
            src_ref=src, dst_ref=dst, send_sem=send, recv_sem=recv,
            device_id=device, device_id_type=MESH,
        ).start()

    def wait_bytes(ref, sem):
        pltpu.make_async_copy(ref, ref, sem).wait()

    loads = [
        pltpu.make_async_copy(src, dst, s_load.at[n])
        for n, (src, dst) in enumerate((
            (o_ref, o_buf), (do_ref, do_buf), (lse_hbm, lse_ref), (wm_hbm, wm_ref), (cf_hbm, cf_ref),
        ))
    ]
    for load in loads:
        load.start()

    barrier = pltpu.get_barrier_semaphore()
    for _, peer, _ in peers:
        pl.semaphore_signal(barrier, inc=1, device_id=(me_c, peer), device_id_type=MESH)
    for side in sides:
        pl.semaphore_signal(barrier, inc=1, device_id=side, device_id_type=MESH)
    pl.semaphore_wait(barrier, len(peers) + len(sides))

    def send_in(head, first, refs, sem):
        for index, ref in enumerate(refs):
            for _, peer, peer_group in peers:
                remote(
                    ref.at[:, columns(peer_group, head)],
                    own.at[head, first + index, my_rows],
                    s_in.at[head], sem.at[head], (me_c, peer),
                )
            pltpu.make_async_copy(
                ref.at[:, columns(group, head)],
                own.at[head, first + index, my_rows],
                sem.at[head],
            ).start()

    def send_queries(head):
        send_in(head, 0, (q_ref, do_ref), r_q)

    def send_keys(head):
        send_in(head, 2, (k_ref, v_ref), r_kv)

    send_queries(0)

    for load in loads:
        load.wait()
    all_heads = groups * heads
    lane = lax.broadcasted_iota(jnp.int32, (tokens, HD), 1)
    columns_f = jnp.zeros((tokens, HD), jnp.float32)
    for n in range(all_heads):
        span = slice(n * HD, (n + 1) * HD)
        product = do_buf[:, span].astype(jnp.float32) * o_buf[:, span].astype(jnp.float32)
        columns_f = jnp.where(lane == n, jnp.sum(product, axis=1, keepdims=True), columns_f)
    rows[...] = columns_f
    turned = rows[...].T
    send_keys(0)
    send_queries(1)
    for g in range(groups):
        stat_send[g] = jnp.zeros((16, tokens), jnp.float32)
        stat_send[g, 0:heads] = lse_ref[g * heads:(g + 1) * heads] * LOG2E
        stat_send[g, 8:8 + heads] = turned[g * heads:(g + 1) * heads]
    stat[me_j] = stat_send[group]
    for _, peer, peer_group in peers:
        remote(stat_send.at[peer_group], stat.at[me_j], s_stat, r_stat, (me_c, peer))

    tiles = 2 * ctx_count

    def tile_at(shift):
        return lax.rem(2 * me_c + shift + tiles, tiles)

    def off_amount(shift_q, shift_k):
        e = shift_k - shift_q + WIN
        s, u = tile_at(shift_q), tile_at(shift_k)
        open_ctx = (cf_ref[s] == 0) | (cf_ref[u] == 1)
        ok = open_ctx if e == WIN else open_ctx & (wm_ref[e, s] == 1)
        return jnp.where(ok, jnp.float32(0.0), jnp.float32(OFF))

    off = {
        (s, u): off_amount(s, u) for s in range(-2, 4) for u in (0, 1) if abs(s - u) <= WIN
    }

    scale = HD ** -0.5

    def stat_row(ref_at, tile, row):
        return jnp.concatenate(
            [ref_at(2 * tile, row), ref_at(2 * tile + 1, row)], axis=1
        )

    def pair(k, v, kt, q, do, lse, delta):
        probs = jnp.exp2(
            lax.dot_general(k, q, NT, preferred_element_type=jnp.float32) * (scale * LOG2E) - lse
        )
        dprobs = lax.dot_general(v, do, NT, preferred_element_type=jnp.float32)
        dscores = (probs * (dprobs - delta)).astype(jnp.bfloat16)
        return (
            matmul(dscores, q),
            matmul(probs.astype(jnp.bfloat16), do),
            matmul(kt, dscores),
        )

    def load_keys(head):
        made = []
        for t in range(2):
            span = pl.ds(t * TILE, TILE)
            k = own[head, 2, span]
            made.append((k, own[head, 3, span], k.T))
        return made

    def own_pairs(head):
        keys = load_keys(head)
        for s in range(2):
            span = pl.ds(s * TILE, TILE)
            q, do = own[head, 0, span], own[head, 1, span]
            row = lambda b, r: stat[b, pl.ds(r, 1)]
            lse, delta = stat_row(row, s, head), stat_row(row, s, head + 8)
            dq = None
            for t in range(2):
                dk, dv, term = pair(*keys[t], q, do, lse + off[s, t], delta)
                if s == 0:
                    acc_kv[0, t], acc_kv[1, t] = dk, dv
                else:
                    acc_kv[0, t] += dk
                    acc_kv[1, t] += dv
                dq = term if dq is None else dq + term
            acc_q[head, s] = dq

    def halo_pairs(head):
        keys = load_keys(head)
        for side in range(2):
            for s in range(2):
                shift = s - 2 if side == 0 else s + 2
                span = pl.ds(s * TILE, TILE)
                q, do = halo[head, side, 0, span], halo[head, side, 1, span]
                row = lambda b, r: stat_halo[side, b, pl.ds(r, 1)]
                lse, delta = stat_row(row, s, head), stat_row(row, s, head + 8)
                dq = None
                for t in range(2):
                    if (shift, t) not in off:
                        continue
                    dk, dv, term = pair(*keys[t], q, do, lse + off[shift, t], delta)
                    acc_kv[0, t] += dk
                    acc_kv[1, t] += dv
                    dq = term if dq is None else dq + term
                part_send[head, side, s] = (dq * scale).astype(jnp.bfloat16)
            remote(
                part_send.at[head, side], part.at[head, 1 - side],
                s_part.at[head], r_part.at[head], sides[side],
            )
        for t in range(2):
            span = pl.ds(t * TILE, TILE)
            out[head, 1, span] = (acc_kv[0, t] * scale).astype(jnp.bfloat16)
            out[head, 2, span] = acc_kv[1, t].astype(jnp.bfloat16)

    outputs = (dq_ref, dk_ref, dv_ref)

    def send_out(head, which):
        for index in which:
            target = outputs[index].at[:, columns(group, head)]
            for _, peer, _ in peers:
                rows_there = pl.ds(pl.multiple_of(peer * tokens, tokens), tokens)
                remote(
                    out.at[head, index, rows_there], target,
                    s_out.at[head], r_out.at[index], (me_c, peer),
                )
            pltpu.make_async_copy(out.at[head, index, my_rows], target, r_out.at[index]).start()

    def finish_q(head):
        for s in range(2):
            total = acc_q[head, s] * scale
            total = total + part[head, 0, s].astype(jnp.float32)
            total = total + part[head, 1, s].astype(jnp.float32)
            out[head, 0, pl.ds(s * TILE, TILE)] = total.T.astype(jnp.bfloat16)

    def step(i, carry):
        @pl.when(i < heads)
        def _():
            wait_bytes(own.at[i, 0:2], r_q.at[i])
            for side in range(2):
                remote(
                    own.at[i, 0:2], halo.at[i, 1 - side],
                    s_halo.at[i], r_halo.at[i, 1 - side], sides[side],
                )

        @pl.when(i + 1 < heads)
        def _():
            send_keys(i + 1)

        @pl.when(i + 2 < heads)
        def _():
            send_queries(i + 2)

        @pl.when(i == 0)
        def _():
            wait_bytes(stat.at[0:3], r_stat)
            for side in range(2):
                remote(stat, stat_halo.at[1 - side], s_hstat, r_hstat.at[1 - side], sides[side])

        @pl.when(i == 1)
        def _():
            for side in range(2):
                wait_bytes(stat_halo.at[side], r_hstat.at[side])

        @pl.when((i >= 1) & (i <= heads))
        def _():
            head = i - 1
            wait_bytes(own.at[head, 2:4], r_kv.at[head])
            own_pairs(head)
            for side in range(2):
                wait_bytes(halo.at[head, side], r_halo.at[head, side])
            halo_pairs(head)
            send_out(head, (1, 2))

        @pl.when(i >= 2)
        def _():
            head = i - 2
            wait_bytes(part.at[head], r_part.at[head])
            finish_q(head)
            send_out(head, (0,))

        return carry

    lax.fori_loop(0, heads + 2, step, 0)

    wait_bytes(stat.at[0:3], s_stat)
    wait_bytes(stat_halo, s_hstat)

    def drain(head, carry):
        wait_bytes(own.at[head, :, pl.ds(0, 3 * tokens)], s_in.at[head])
        wait_bytes(own.at[head], s_halo.at[head])
        wait_bytes(part_send.at[head], s_part.at[head])
        wait_bytes(out.at[head, :, pl.ds(0, 3 * tokens)], s_out.at[head])
        return carry

    lax.fori_loop(0, heads, drain, 0)
    for index in range(3):
        wait_bytes(outputs[index], r_out.at[index])


def copy_out(*refs):
    buf, sems = refs[6], refs[7]
    parts = 4
    size = refs[0].shape[0] // parts
    steps = [(n, p, pl.ds(p * size, size)) for p in range(parts) for n in range(3)]
    ins = [pltpu.make_async_copy(refs[n].at[r], buf.at[n, r], sems.at[0, n, p]) for n, p, r in steps]
    outs = [pltpu.make_async_copy(buf.at[n, r], refs[3 + n].at[r], sems.at[1, n, p]) for n, p, r in steps]
    for copy in ins:
        copy.start()
    for first, second in zip(ins, outs):
        first.wait()
        second.start()
    for copy in outs:
        copy.wait()


def per_device(queries, keys, values, outputs, out_grads, log_sums, window_mask, context_flag):
    tokens, width = queries.shape
    ctx_count, groups = lax.axis_size("ctx"), lax.axis_size("head")
    heads = log_sums.shape[1] // groups
    block = groups * tokens
    bf16, f32 = jnp.bfloat16, jnp.float32
    dma, vmem = pltpu.SemaphoreType.DMA, pltpu.VMEM
    anywhere = pl.BlockSpec(memory_space=pl.ANY)
    grads = pl.pallas_call(
        functools.partial(kernel, ctx_count, heads),
        out_shape=[jax.ShapeDtypeStruct((tokens, width), bf16)] * 3,
        in_specs=[anywhere] * 8,
        out_specs=[anywhere] * 3,
        scratch_shapes=[
            vmem((heads, 4, block, HD), bf16),
            vmem((heads, 2, 2, block, HD), bf16),
            vmem((groups, 16, tokens), f32),
            vmem((groups, 16, tokens), f32),
            vmem((2, groups, 16, tokens), f32),
            vmem((tokens, width), bf16),
            vmem((tokens, width), bf16),
            vmem(log_sums.shape[::-1], f32),
            pltpu.SMEM(window_mask.shape[::-1], jnp.int32),
            pltpu.SMEM(context_flag.shape, jnp.int32),
            vmem((tokens, HD), f32),
            vmem((2, 2, TILE, HD), f32),
            vmem((heads, 2, HD, TILE), f32),
            vmem((heads, 2, 2, HD, TILE), bf16),
            vmem((heads, 2, 2, HD, TILE), bf16),
            vmem((heads, 3, block, HD), bf16),
            dma((5,)),
            dma((heads,)),
            dma((heads,)),
            dma((heads,)),
            dma,
            dma,
            dma,
            dma((2,)),
            dma((heads,)),
            dma((heads, 2)),
            dma((heads,)),
            dma((heads,)),
            dma((heads,)),
            dma((3,)),
        ],
        compiler_params=pltpu.CompilerParams(
            collective_id=0, has_side_effects=True, vmem_limit_bytes=60 * 1024 * 1024
        ),
        name="attention_grads",
    )(queries, keys, values, outputs, out_grads, log_sums.T, window_mask.T, context_flag)
    return pl.pallas_call(
        copy_out,
        out_shape=[jax.ShapeDtypeStruct((tokens, width), bf16)] * 3,
        in_specs=[anywhere] * 3,
        out_specs=[anywhere] * 3,
        scratch_shapes=[vmem((3, tokens, width), bf16), dma((2, 3, 4))],
        name="results_out",
    )(*grads)


def solution(mesh):
    placed = (P(("ctx", "head"), None),) * 6 + (P(), P())
    return jax.shard_map(
        per_device,
        mesh=mesh,
        in_specs=placed,
        out_specs=(P(("ctx", "head"), None),) * 3,
        check_vma=False,
    )
```

```python
import functools

import jax
import jax.numpy as jnp
from jax import lax
from jax.experimental import pallas as pl
from jax.experimental.pallas import tpu as pltpu
from jax.sharding import PartitionSpec as P

TILE = 256
HD = 128
WIN = 2
LOG2E = 1.4426950408889634
OFF = 1e30
FIRST_DELTAS = 10
MESH = pl.DeviceIdType.MESH
NT = (((1,), (1,)), ((), ()))


def matmul(a, b):
    return jnp.dot(a, b, preferred_element_type=jnp.float32)


def kernel(
    ctx_count,
    heads,
    q_ref, k_ref, v_ref, o_ref, do_ref, lse_hbm, wm_hbm, cf_hbm,
    dq_ref, dk_ref, dv_ref,
    own, halo, stat_send, stat, stat_halo, o_buf, do_buf, lse_ref, wm_ref, cf_ref, rows,
    acc_kv, acc_q, part_send, part, out,
    s_load, s_in, r_q, r_kv, s_stat, r_stat, s_hstat, r_hstat, s_halo, r_halo,
    s_part, r_part, s_out, r_out, gate,
):
    tokens = q_ref.shape[0]
    groups = 4
    me_c, me_j = lax.axis_index("ctx"), lax.axis_index("head")
    half = ctx_count // 2
    flip = me_c // half
    group = lax.rem(me_j + 2 * flip, groups)
    sides = []
    for step in (ctx_count - 1, 1):
        c = lax.rem(me_c + step, ctx_count)
        sides.append((c, lax.rem(me_j + 2 * flip + 2 * (c // half), groups)))
    peers = [(r, lax.rem(me_j + r, groups), lax.rem(group + r, groups)) for r in (2, 1, 3)]
    my_rows = pl.ds(pl.multiple_of(me_j * tokens, tokens), tokens)

    def columns(which_group, head):
        return pl.ds(pl.multiple_of((which_group * heads + head) * HD, HD), HD)

    def remote(src, dst, send, recv, device):
        pltpu.make_async_remote_copy(
            src_ref=src, dst_ref=dst, send_sem=send, recv_sem=recv,
            device_id=device, device_id_type=MESH,
        ).start()

    def wait_bytes(ref, sem):
        pltpu.make_async_copy(ref, ref, sem).wait()

    loads = [
        pltpu.make_async_copy(src, dst, s_load.at[n])
        for n, (src, dst) in enumerate((
            (o_ref, o_buf), (do_ref, do_buf), (lse_hbm, lse_ref), (wm_hbm, wm_ref), (cf_hbm, cf_ref),
        ))
    ]
    for load in loads:
        load.start()

    leader = groups - 1
    barrier = pltpu.get_barrier_semaphore()
    for _, peer, peer_group in peers:
        @pl.when(peer_group != leader)
        def _():
            pl.semaphore_signal(barrier, inc=1, device_id=(me_c, peer), device_id_type=MESH)

    for c, _ in sides:
        side_leader = lax.rem(leader + 2 * (c // half), groups)
        pl.semaphore_signal(barrier, inc=1, device_id=(c, side_leader), device_id_type=MESH)

    @pl.when(group != leader)
    def _():
        pl.semaphore_wait(barrier, len(peers))

    for _, peer, peer_group in peers:
        @pl.when(peer_group == leader)
        def _():
            pl.semaphore_signal(gate, inc=1, device_id=(me_c, peer), device_id_type=MESH)

    @pl.when(group == leader)
    def _():
        pl.semaphore_wait(gate, len(peers))

    def meet_sides():
        @pl.when(group == leader)
        def _():
            pl.semaphore_wait(barrier, len(sides) * groups)
            for _, peer, _ in peers:
                pl.semaphore_signal(gate, inc=1, device_id=(me_c, peer), device_id_type=MESH)

        @pl.when(group != leader)
        def _():
            pl.semaphore_wait(gate, 1)

    def send_in(head, first, refs, sem):
        for index, ref in enumerate(refs):
            for _, peer, peer_group in peers:
                remote(
                    ref.at[:, columns(peer_group, head)],
                    own.at[head, first + index, my_rows],
                    s_in.at[head], sem.at[head], (me_c, peer),
                )
            pltpu.make_async_copy(
                ref.at[:, columns(group, head)],
                own.at[head, first + index, my_rows],
                sem.at[head],
            ).start()

    def send_queries(head):
        send_in(head, 0, (q_ref, do_ref), r_q)

    def send_keys(head):
        send_in(head, 2, (k_ref, v_ref), r_kv)

    send_queries(0)

    partner_rows = pl.ds(pl.multiple_of((1 - me_j // 2) * TILE, TILE), TILE)

    def send_halo_direct(head):
        for index, ref in enumerate((q_ref, do_ref)):
            for core in range(2):
                their_group = group + core * (1 - 2 * lax.rem(group, 2))
                for side, (c, j) in enumerate(sides):
                    remote(
                        ref.at[:, columns(their_group, head)],
                        halo.at[head, 1 - side, index, my_rows],
                        s_halo.at[head], r_halo.at[head, 1 - side],
                        (c, j + core * (1 - 2 * lax.rem(j, 2))),
                    )

    def send_halo(head):
        wait_bytes(own.at[head, 0:2], r_q.at[head])
        for side in range(2):
            remote(
                own.at[head, 0:2, partner_rows], halo.at[head, 1 - side, :, partner_rows],
                s_halo.at[head], r_halo.at[head, 1 - side], sides[side],
            )

    all_heads = groups * heads
    lane = lax.broadcasted_iota(jnp.int32, (tokens, HD), 1)

    def add_deltas(columns_f, first, last):
        for n in range(first, last):
            span = slice(n * HD, (n + 1) * HD)
            product = do_buf[:, span].astype(jnp.float32) * o_buf[:, span].astype(jnp.float32)
            columns_f = jnp.where(lane == n, jnp.sum(product, axis=1, keepdims=True), columns_f)
        return columns_f

    for load in loads:
        load.wait()
    rows[...] = add_deltas(jnp.zeros((tokens, HD), jnp.float32), 0, FIRST_DELTAS)
    send_keys(0)
    meet_sides()
    send_halo_direct(0)
    send_halo(0)
    send_halo_direct(1)
    send_queries(1)
    turned = add_deltas(rows[...], FIRST_DELTAS, all_heads).T
    for g in range(groups):
        stat_send[g] = jnp.zeros((16, tokens), jnp.float32)
        stat_send[g, 0:heads] = lse_ref[g * heads:(g + 1) * heads] * LOG2E
        stat_send[g, 8:8 + heads] = turned[g * heads:(g + 1) * heads]
    stat[me_j] = stat_send[group]
    for _, peer, peer_group in peers:
        remote(stat_send.at[peer_group], stat.at[me_j], s_stat, r_stat, (me_c, peer))
    send_keys(1)
    send_queries(2)
    wait_bytes(stat.at[0:3], r_stat)
    for side in range(2):
        remote(stat, stat_halo.at[1 - side], s_hstat, r_hstat.at[1 - side], sides[side])

    tiles = 2 * ctx_count

    def tile_at(shift):
        return lax.rem(2 * me_c + shift + tiles, tiles)

    def off_amount(shift_q, shift_k):
        e = shift_k - shift_q + WIN
        s, u = tile_at(shift_q), tile_at(shift_k)
        open_ctx = (cf_ref[s] == 0) | (cf_ref[u] == 1)
        ok = open_ctx if e == WIN else open_ctx & (wm_ref[e, s] == 1)
        return jnp.where(ok, jnp.float32(0.0), jnp.float32(OFF))

    off = {
        (s, u): off_amount(s, u) for s in range(-2, 4) for u in (0, 1) if abs(s - u) <= WIN
    }

    scale = HD ** -0.5

    def stat_row(ref_at, tile, row):
        return jnp.concatenate(
            [ref_at(2 * tile, row), ref_at(2 * tile + 1, row)], axis=1
        )

    def pair(k, v, kt, q, do, lse, delta):
        probs = jnp.exp2(
            lax.dot_general(k, q, NT, preferred_element_type=jnp.float32) * (scale * LOG2E) - lse
        )
        dprobs = lax.dot_general(v, do, NT, preferred_element_type=jnp.float32)
        dscores = (probs * (dprobs - delta)).astype(jnp.bfloat16)
        return (
            matmul(dscores, q),
            matmul(probs.astype(jnp.bfloat16), do),
            matmul(kt, dscores),
        )

    def load_keys(head):
        made = []
        for t in range(2):
            span = pl.ds(t * TILE, TILE)
            k = own[head, 2, span]
            made.append((k, own[head, 3, span], k.T))
        return made

    def own_pairs(head):
        keys = load_keys(head)
        for s in range(2):
            span = pl.ds(s * TILE, TILE)
            q, do = own[head, 0, span], own[head, 1, span]
            row = lambda b, r: stat[b, pl.ds(r, 1)]
            lse, delta = stat_row(row, s, head), stat_row(row, s, head + 8)
            dq = None
            for t in range(2):
                dk, dv, term = pair(*keys[t], q, do, lse + off[s, t], delta)
                if s == 0:
                    acc_kv[0, t], acc_kv[1, t] = dk, dv
                else:
                    acc_kv[0, t] += dk
                    acc_kv[1, t] += dv
                dq = term if dq is None else dq + term
            acc_q[head, s] = dq

    def halo_pairs(head):
        keys = load_keys(head)
        for side in range(2):
            for s in range(2):
                shift = s - 2 if side == 0 else s + 2
                span = pl.ds(s * TILE, TILE)
                q, do = halo[head, side, 0, span], halo[head, side, 1, span]
                row = lambda b, r: stat_halo[side, b, pl.ds(r, 1)]
                lse, delta = stat_row(row, s, head), stat_row(row, s, head + 8)
                dq = None
                for t in range(2):
                    if (shift, t) not in off:
                        continue
                    dk, dv, term = pair(*keys[t], q, do, lse + off[shift, t], delta)
                    acc_kv[0, t] += dk
                    acc_kv[1, t] += dv
                    dq = term if dq is None else dq + term
                part_send[head, side, s] = (dq * scale).astype(jnp.bfloat16)
                remote(
                    part_send.at[head, side, s], part.at[head, 1 - side, s],
                    s_part.at[head], r_part.at[head, s], sides[side],
                )
        for t in range(2):
            span = pl.ds(t * TILE, TILE)
            out[head, 1, span] = (acc_kv[0, t] * scale).astype(jnp.bfloat16)
            out[head, 2, span] = acc_kv[1, t].astype(jnp.bfloat16)

    outputs = (dq_ref, dk_ref, dv_ref)

    def send_out(head, which):
        for index in which:
            target = outputs[index].at[:, columns(group, head)]
            for _, peer, _ in peers:
                rows_there = pl.ds(pl.multiple_of(peer * tokens, tokens), tokens)
                remote(
                    out.at[head, index, rows_there], target,
                    s_out.at[head], r_out.at[index], (me_c, peer),
                )
            pltpu.make_async_copy(out.at[head, index, my_rows], target, r_out.at[index]).start()

    def finish_q(head):
        for s in range(2):
            wait_bytes(part.at[head, :, s], r_part.at[head, s])
            total = acc_q[head, s] * scale
            total = total + part[head, 0, s].astype(jnp.float32)
            total = total + part[head, 1, s].astype(jnp.float32)
            out[head, 0, pl.ds(s * TILE, TILE)] = total.T.astype(jnp.bfloat16)
            target = outputs[0].at[:, columns(group, head)]
            for peer in (2 * s, 2 * s + 1):
                source = out.at[head, 0, pl.ds(peer * tokens, tokens)]

                @pl.when(peer != me_j)
                def _():
                    remote(source, target, s_out.at[head], r_out.at[0], (me_c, peer))

                @pl.when(peer == me_j)
                def _():
                    pltpu.make_async_copy(source, target, r_out.at[0]).start()

    def step(i, carry):
        @pl.when(i < heads)
        def _():
            send_halo(i)

        @pl.when(i + 1 < heads)
        def _():
            send_halo_direct(i + 1)

        @pl.when(i + 1 < heads)
        def _():
            send_keys(i + 1)

        @pl.when(i + 2 < heads)
        def _():
            send_queries(i + 2)

        @pl.when(i == 1)
        def _():
            for side in range(2):
                wait_bytes(stat_halo.at[side], r_hstat.at[side])

        @pl.when(i <= heads)
        def _():
            head = i - 1
            wait_bytes(own.at[head, 2:4], r_kv.at[head])
            own_pairs(head)
            for side in range(2):
                wait_bytes(halo.at[head, side], r_halo.at[head, side])
            halo_pairs(head)
            send_out(head, (1, 2))

        @pl.when(i >= 2)
        def _():
            head = i - 2
            finish_q(head)

        return carry

    lax.fori_loop(1, heads + 2, step, 0)

    wait_bytes(stat.at[0:3], s_stat)
    wait_bytes(stat_halo, s_hstat)

    def drain(head, carry):
        wait_bytes(own.at[head, :, pl.ds(0, 3 * tokens)], s_in.at[head])
        wait_bytes(own.at[head], s_halo.at[head])
        wait_bytes(part_send.at[head], s_part.at[head])
        wait_bytes(out.at[head, :, pl.ds(0, 3 * tokens)], s_out.at[head])
        return carry

    lax.fori_loop(0, heads, drain, 0)
    for index in range(3):
        wait_bytes(outputs[index], r_out.at[index])


def copy_out(*refs):
    buf, sems = refs[6], refs[7]
    parts = 4
    size = refs[0].shape[0] // parts
    steps = [(n, p, pl.ds(p * size, size)) for p in range(parts) for n in range(3)]
    ins = [pltpu.make_async_copy(refs[n].at[r], buf.at[n, r], sems.at[0, n, p]) for n, p, r in steps]
    outs = [pltpu.make_async_copy(buf.at[n, r], refs[3 + n].at[r], sems.at[1, n, p]) for n, p, r in steps]
    for copy in ins:
        copy.start()
    for first, second in zip(ins, outs):
        first.wait()
        second.start()
    for copy in outs:
        copy.wait()


def per_device(queries, keys, values, outputs, out_grads, log_sums, window_mask, context_flag):
    tokens, width = queries.shape
    ctx_count, groups = lax.axis_size("ctx"), lax.axis_size("head")
    heads = log_sums.shape[1] // groups
    block = groups * tokens
    bf16, f32 = jnp.bfloat16, jnp.float32
    dma, vmem = pltpu.SemaphoreType.DMA, pltpu.VMEM
    anywhere = pl.BlockSpec(memory_space=pl.ANY)
    grads = pl.pallas_call(
        functools.partial(kernel, ctx_count, heads),
        out_shape=[jax.ShapeDtypeStruct((tokens, width), bf16)] * 3,
        in_specs=[anywhere] * 8,
        out_specs=[anywhere] * 3,
        scratch_shapes=[
            vmem((heads, 4, block, HD), bf16),
            vmem((heads, 2, 2, block, HD), bf16),
            vmem((groups, 16, tokens), f32),
            vmem((groups, 16, tokens), f32),
            vmem((2, groups, 16, tokens), f32),
            vmem((tokens, width), bf16),
            vmem((tokens, width), bf16),
            vmem(log_sums.shape[::-1], f32),
            pltpu.SMEM(window_mask.shape[::-1], jnp.int32),
            pltpu.SMEM(context_flag.shape, jnp.int32),
            vmem((tokens, HD), f32),
            vmem((2, 2, TILE, HD), f32),
            vmem((heads, 2, HD, TILE), f32),
            vmem((heads, 2, 2, HD, TILE), bf16),
            vmem((heads, 2, 2, HD, TILE), bf16),
            vmem((heads, 3, block, HD), bf16),
            dma((5,)),
            dma((heads,)),
            dma((heads,)),
            dma((heads,)),
            dma,
            dma,
            dma,
            dma((2,)),
            dma((heads,)),
            dma((heads, 2)),
            dma((heads,)),
            dma((heads, 2)),
            dma((heads,)),
            dma((3,)),
            pltpu.SemaphoreType.REGULAR,
        ],
        compiler_params=pltpu.CompilerParams(
            collective_id=0, has_side_effects=True, vmem_limit_bytes=60 * 1024 * 1024
        ),
        name="attention_grads",
    )(queries, keys, values, outputs, out_grads, log_sums.T, window_mask.T, context_flag)
    return pl.pallas_call(
        copy_out,
        out_shape=[jax.ShapeDtypeStruct((tokens, width), bf16)] * 3,
        in_specs=[anywhere] * 3,
        out_specs=[anywhere] * 3,
        scratch_shapes=[vmem((3, tokens, width), bf16), dma((2, 3, 4))],
        name="results_out",
    )(*grads)


def solution(mesh):
    placed = (P(("ctx", "head"), None),) * 6 + (P(), P())
    return jax.shard_map(
        per_device,
        mesh=mesh,
        in_specs=placed,
        out_specs=(P(("ctx", "head"), None),) * 3,
        check_vma=False,
    )
```

```python
import functools

import jax
import jax.numpy as jnp
from jax import lax
from jax.experimental import pallas as pl
from jax.experimental.pallas import tpu as pltpu
from jax.sharding import PartitionSpec as P

TILE = 256
HD = 128
WIN = 2
LOG2E = 1.4426950408889634
OFF = 1e30
FIRST_DELTAS = 10
MESH = pl.DeviceIdType.MESH
NT = (((1,), (1,)), ((), ()))


def matmul(a, b):
    return jnp.dot(a, b, preferred_element_type=jnp.float32)


def kernel(
    ctx_count,
    heads,
    q_ref, k_ref, v_ref, o_ref, do_ref, lse_hbm, wm_hbm, cf_hbm,
    dq_ref, dk_ref, dv_ref,
    own, halo, stat_send, stat, stat_halo, o_buf, do_buf, lse_ref, wm_ref, cf_ref, rows,
    acc_kv, acc_q, part_send, part, out,
    s_load, s_in, r_q, r_kv, s_stat, r_stat, s_hstat, r_hstat, s_halo, r_halo,
    s_part, r_part, s_out, r_out, gate,
):
    tokens = q_ref.shape[0]
    groups = 4
    me_c, me_j = lax.axis_index("ctx"), lax.axis_index("head")
    half = ctx_count // 2
    flip = me_c // half
    group = lax.rem(me_j + 2 * flip, groups)
    sides = []
    for step in (ctx_count - 1, 1):
        c = lax.rem(me_c + step, ctx_count)
        sides.append((c, lax.rem(me_j + 2 * flip + 2 * (c // half), groups)))
    peers = [(r, lax.rem(me_j + r, groups), lax.rem(group + r, groups)) for r in (2, 1, 3)]
    my_rows = pl.ds(pl.multiple_of(me_j * tokens, tokens), tokens)

    def columns(which_group, head):
        return pl.ds(pl.multiple_of((which_group * heads + head) * HD, HD), HD)

    def remote(src, dst, send, recv, device):
        pltpu.make_async_remote_copy(
            src_ref=src, dst_ref=dst, send_sem=send, recv_sem=recv,
            device_id=device, device_id_type=MESH,
        ).start()

    def wait_bytes(ref, sem):
        pltpu.make_async_copy(ref, ref, sem).wait()

    loads = [
        pltpu.make_async_copy(src, dst, s_load.at[n])
        for n, (src, dst) in enumerate((
            (o_ref, o_buf), (do_ref, do_buf), (lse_hbm, lse_ref), (wm_hbm, wm_ref), (cf_hbm, cf_ref),
        ))
    ]
    for load in loads:
        load.start()

    leader = groups - 1
    barrier = pltpu.get_barrier_semaphore()
    for _, peer, peer_group in peers:
        @pl.when(peer_group != leader)
        def _():
            pl.semaphore_signal(barrier, inc=1, device_id=(me_c, peer), device_id_type=MESH)

    for c, _ in sides:
        side_leader = lax.rem(leader + 2 * (c // half), groups)
        pl.semaphore_signal(barrier, inc=1, device_id=(c, side_leader), device_id_type=MESH)

    @pl.when(group != leader)
    def _():
        pl.semaphore_wait(barrier, len(peers))

    for _, peer, peer_group in peers:
        @pl.when(peer_group == leader)
        def _():
            pl.semaphore_signal(gate, inc=1, device_id=(me_c, peer), device_id_type=MESH)

    @pl.when(group == leader)
    def _():
        pl.semaphore_wait(gate, len(peers))

    def meet_sides():
        @pl.when(group == leader)
        def _():
            pl.semaphore_wait(barrier, len(sides) * groups)
            for _, peer, _ in peers:
                pl.semaphore_signal(gate, inc=1, device_id=(me_c, peer), device_id_type=MESH)

        @pl.when(group != leader)
        def _():
            pl.semaphore_wait(gate, 1)

    def send_in(head, first, refs, sem):
        for index, ref in enumerate(refs):
            for _, peer, peer_group in peers:
                remote(
                    ref.at[:, columns(peer_group, head)],
                    own.at[head, first + index, my_rows],
                    s_in.at[head], sem.at[head], (me_c, peer),
                )
            pltpu.make_async_copy(
                ref.at[:, columns(group, head)],
                own.at[head, first + index, my_rows],
                sem.at[head],
            ).start()

    def send_queries(head):
        send_in(head, 0, (q_ref, do_ref), r_q)

    def send_keys(head):
        send_in(head, 2, (k_ref, v_ref), r_kv)

    send_queries(0)

    partner_rows = pl.ds(pl.multiple_of((1 - me_j // 2) * TILE, TILE), TILE)

    def send_halo_direct(head):
        for index, ref in enumerate((q_ref, do_ref)):
            for core in range(2):
                their_group = group + core * (1 - 2 * lax.rem(group, 2))
                for side, (c, j) in enumerate(sides):
                    remote(
                        ref.at[:, columns(their_group, head)],
                        halo.at[head, 1 - side, index, my_rows],
                        s_halo.at[head], r_halo.at[head, 1 - side],
                        (c, j + core * (1 - 2 * lax.rem(j, 2))),
                    )

    def send_halo(head):
        wait_bytes(own.at[head, 0:2], r_q.at[head])
        for side in range(2):
            remote(
                own.at[head, 0:2, partner_rows], halo.at[head, 1 - side, :, partner_rows],
                s_halo.at[head], r_halo.at[head, 1 - side], sides[side],
            )

    all_heads = groups * heads
    lane = lax.broadcasted_iota(jnp.int32, (tokens, HD), 1)

    def add_deltas(columns_f, first, last):
        for n in range(first, last):
            span = slice(n * HD, (n + 1) * HD)
            product = do_buf[:, span].astype(jnp.float32) * o_buf[:, span].astype(jnp.float32)
            columns_f = jnp.where(lane == n, jnp.sum(product, axis=1, keepdims=True), columns_f)
        return columns_f

    for load in loads:
        load.wait()
    rows[...] = add_deltas(jnp.zeros((tokens, HD), jnp.float32), 0, FIRST_DELTAS)
    send_keys(0)
    meet_sides()
    send_halo_direct(0)
    send_halo(0)
    send_queries(1)
    send_halo_direct(1)
    turned = add_deltas(rows[...], FIRST_DELTAS, all_heads).T
    for g in range(groups):
        stat_send[g] = jnp.zeros((16, tokens), jnp.float32)
        stat_send[g, 0:heads] = lse_ref[g * heads:(g + 1) * heads] * LOG2E
        stat_send[g, 8:8 + heads] = turned[g * heads:(g + 1) * heads]
    stat[me_j] = stat_send[group]
    for _, peer, peer_group in peers:
        remote(stat_send.at[peer_group], stat.at[me_j], s_stat, r_stat, (me_c, peer))
    send_queries(2)
    send_halo(1)
    send_halo_direct(2)
    send_keys(1)
    send_queries(3)
    wait_bytes(stat.at[0:3], r_stat)
    for side in range(2):
        remote(stat, stat_halo.at[1 - side], s_hstat, r_hstat.at[1 - side], sides[side])

    tiles = 2 * ctx_count

    def tile_at(shift):
        return lax.rem(2 * me_c + shift + tiles, tiles)

    def off_amount(shift_q, shift_k):
        e = shift_k - shift_q + WIN
        s, u = tile_at(shift_q), tile_at(shift_k)
        open_ctx = (cf_ref[s] == 0) | (cf_ref[u] == 1)
        ok = open_ctx if e == WIN else open_ctx & (wm_ref[e, s] == 1)
        return jnp.where(ok, jnp.float32(0.0), jnp.float32(OFF))

    off = {
        (s, u): off_amount(s, u) for s in range(-2, 4) for u in (0, 1) if abs(s - u) <= WIN
    }

    scale = HD ** -0.5

    def stat_row(ref_at, tile, row):
        return jnp.concatenate(
            [ref_at(2 * tile, row), ref_at(2 * tile + 1, row)], axis=1
        )

    def pair(k, v, kt, q, do, lse, delta):
        probs = jnp.exp2(
            lax.dot_general(k, q, NT, preferred_element_type=jnp.float32) * (scale * LOG2E) - lse
        )
        dprobs = lax.dot_general(v, do, NT, preferred_element_type=jnp.float32)
        dscores = (probs * (dprobs - delta)).astype(jnp.bfloat16)
        return (
            matmul(dscores, q),
            matmul(probs.astype(jnp.bfloat16), do),
            matmul(kt, dscores),
        )

    def load_keys(head):
        made = []
        for t in range(2):
            span = pl.ds(t * TILE, TILE)
            k = own[head, 2, span]
            made.append((k, own[head, 3, span], k.T))
        return made

    def own_pairs(head):
        keys = load_keys(head)
        for s in range(2):
            span = pl.ds(s * TILE, TILE)
            q, do = own[head, 0, span], own[head, 1, span]
            row = lambda b, r: stat[b, pl.ds(r, 1)]
            lse, delta = stat_row(row, s, head), stat_row(row, s, head + 8)
            dq = None
            for t in range(2):
                dk, dv, term = pair(*keys[t], q, do, lse + off[s, t], delta)
                if s == 0:
                    acc_kv[0, t], acc_kv[1, t] = dk, dv
                else:
                    acc_kv[0, t] += dk
                    acc_kv[1, t] += dv
                dq = term if dq is None else dq + term
            acc_q[head, s] = dq

    def halo_pairs(head):
        keys = load_keys(head)
        for side in range(2):
            for s in range(2):
                shift = s - 2 if side == 0 else s + 2
                span = pl.ds(s * TILE, TILE)
                q, do = halo[head, side, 0, span], halo[head, side, 1, span]
                row = lambda b, r: stat_halo[side, b, pl.ds(r, 1)]
                lse, delta = stat_row(row, s, head), stat_row(row, s, head + 8)
                dq = None
                for t in range(2):
                    if (shift, t) not in off:
                        continue
                    dk, dv, term = pair(*keys[t], q, do, lse + off[shift, t], delta)
                    acc_kv[0, t] += dk
                    acc_kv[1, t] += dv
                    dq = term if dq is None else dq + term
                part_send[head, side, s] = (dq * scale).astype(jnp.bfloat16)
                remote(
                    part_send.at[head, side, s], part.at[head, 1 - side, s],
                    s_part.at[head], r_part.at[head, s], sides[side],
                )
        for t in range(2):
            span = pl.ds(t * TILE, TILE)
            out[head, 1, span] = (acc_kv[0, t] * scale).astype(jnp.bfloat16)
            out[head, 2, span] = acc_kv[1, t].astype(jnp.bfloat16)

    outputs = (dq_ref, dk_ref, dv_ref)

    def send_out(head, which):
        for index in which:
            target = outputs[index].at[:, columns(group, head)]
            for _, peer, _ in peers:
                rows_there = pl.ds(pl.multiple_of(peer * tokens, tokens), tokens)
                remote(
                    out.at[head, index, rows_there], target,
                    s_out.at[head], r_out.at[index], (me_c, peer),
                )
            pltpu.make_async_copy(out.at[head, index, my_rows], target, r_out.at[index]).start()

    def finish_q(head):
        for s in range(2):
            wait_bytes(part.at[head, :, s], r_part.at[head, s])
            total = acc_q[head, s] * scale
            total = total + part[head, 0, s].astype(jnp.float32)
            total = total + part[head, 1, s].astype(jnp.float32)
            out[head, 0, pl.ds(s * TILE, TILE)] = total.T.astype(jnp.bfloat16)
            target = outputs[0].at[:, columns(group, head)]
            for peer in (2 * s, 2 * s + 1):
                source = out.at[head, 0, pl.ds(peer * tokens, tokens)]

                @pl.when(peer != me_j)
                def _():
                    remote(source, target, s_out.at[head], r_out.at[0], (me_c, peer))

                @pl.when(peer == me_j)
                def _():
                    pltpu.make_async_copy(source, target, r_out.at[0]).start()

    def step(i, carry):
        @pl.when(i + 1 < heads)
        def _():
            send_halo(i + 1)
            send_keys(i + 1)

        @pl.when(i + 2 < heads)
        def _():
            send_halo_direct(i + 2)

        @pl.when(i + 3 < heads)
        def _():
            send_queries(i + 3)

        @pl.when(i == 1)
        def _():
            for side in range(2):
                wait_bytes(stat_halo.at[side], r_hstat.at[side])

        @pl.when(i <= heads)
        def _():
            head = i - 1
            wait_bytes(own.at[head, 2:4], r_kv.at[head])
            own_pairs(head)
            for side in range(2):
                wait_bytes(halo.at[head, side], r_halo.at[head, side])
            halo_pairs(head)
            send_out(head, (1, 2))

        @pl.when(i >= 3)
        def _():
            head = i - 3
            finish_q(head)

        return carry

    lax.fori_loop(1, heads + 3, step, 0)

    wait_bytes(stat.at[0:3], s_stat)
    wait_bytes(stat_halo, s_hstat)

    def drain(head, carry):
        wait_bytes(own.at[head, :, pl.ds(0, 3 * tokens)], s_in.at[head])
        wait_bytes(own.at[head], s_halo.at[head])
        wait_bytes(part_send.at[head], s_part.at[head])
        wait_bytes(out.at[head, :, pl.ds(0, 3 * tokens)], s_out.at[head])
        return carry

    lax.fori_loop(0, heads, drain, 0)
    for index in range(3):
        wait_bytes(outputs[index], r_out.at[index])


def copy_out(*refs):
    sems = refs[6]
    copies = [pltpu.make_async_copy(refs[n], refs[3 + n], sems.at[n]) for n in range(3)]
    for copy in copies:
        copy.start()
    for copy in copies:
        copy.wait()


def per_device(queries, keys, values, outputs, out_grads, log_sums, window_mask, context_flag):
    tokens, width = queries.shape
    ctx_count, groups = lax.axis_size("ctx"), lax.axis_size("head")
    heads = log_sums.shape[1] // groups
    block = groups * tokens
    bf16, f32 = jnp.bfloat16, jnp.float32
    dma, vmem = pltpu.SemaphoreType.DMA, pltpu.VMEM
    anywhere = pl.BlockSpec(memory_space=pl.ANY)
    grads = pl.pallas_call(
        functools.partial(kernel, ctx_count, heads),
        out_shape=[vmem((tokens, width), bf16)] * 3,
        in_specs=[anywhere] * 8,
        out_specs=[anywhere] * 3,
        scratch_shapes=[
            vmem((heads, 4, block, HD), bf16),
            vmem((heads, 2, 2, block, HD), bf16),
            vmem((groups, 16, tokens), f32),
            vmem((groups, 16, tokens), f32),
            vmem((2, groups, 16, tokens), f32),
            vmem((tokens, width), bf16),
            vmem((tokens, width), bf16),
            vmem(log_sums.shape[::-1], f32),
            pltpu.SMEM(window_mask.shape[::-1], jnp.int32),
            pltpu.SMEM(context_flag.shape, jnp.int32),
            vmem((tokens, HD), f32),
            vmem((2, 2, TILE, HD), f32),
            vmem((heads, 2, HD, TILE), f32),
            vmem((heads, 2, 2, HD, TILE), bf16),
            vmem((heads, 2, 2, HD, TILE), bf16),
            vmem((heads, 3, block, HD), bf16),
            dma((5,)),
            dma((heads,)),
            dma((heads,)),
            dma((heads,)),
            dma,
            dma,
            dma,
            dma((2,)),
            dma((heads,)),
            dma((heads, 2)),
            dma((heads,)),
            dma((heads, 2)),
            dma((heads,)),
            dma((3,)),
            pltpu.SemaphoreType.REGULAR,
        ],
        compiler_params=pltpu.CompilerParams(
            collective_id=0, has_side_effects=True, vmem_limit_bytes=60 * 1024 * 1024
        ),
        name="attention_grads",
    )(queries, keys, values, outputs, out_grads, log_sums.T, window_mask.T, context_flag)
    return pl.pallas_call(
        copy_out,
        out_shape=[jax.ShapeDtypeStruct((tokens, width), bf16)] * 3,
        in_specs=[pl.BlockSpec(memory_space=pltpu.VMEM)] * 3,
        out_specs=[anywhere] * 3,
        scratch_shapes=[dma((3,))],
        compiler_params=pltpu.CompilerParams(vmem_limit_bytes=8 * 1024 * 1024),
        name="results_out",
    )(*grads)


def solution(mesh):
    placed = (P(("ctx", "head"), None),) * 6 + (P(), P())
    return jax.shard_map(
        per_device,
        mesh=mesh,
        in_specs=placed,
        out_specs=(P(("ctx", "head"), None),) * 3,
        check_vma=False,
    )
```

```python
import functools

import jax
import jax.numpy as jnp
from jax import lax
from jax.experimental import pallas as pl
from jax.experimental.pallas import tpu as pltpu
from jax.sharding import PartitionSpec as P

TILE = 256
HD = 128
WIN = 2
LOG2E = 1.4426950408889634
OFF = 1e30
FIRST_DELTAS = 10
MESH = pl.DeviceIdType.MESH
NT = (((1,), (1,)), ((), ()))


def matmul(a, b):
    return jnp.dot(a, b, preferred_element_type=jnp.float32)


def kernel(
    ctx_count,
    heads,
    q_ref, k_ref, v_ref, o_ref, do_ref, lse_hbm, wm_hbm, cf_hbm,
    dq_ref, dk_ref, dv_ref,
    own, halo, stat_send, stat, stat_halo, o_buf, do_buf, lse_ref, wm_ref, cf_ref, rows,
    acc_kv, acc_q, part_send, part, out,
    s_load, s_in, r_q, r_kv, s_stat, r_stat, s_hstat, r_hstat, s_halo, r_halo,
    s_part, r_part, s_out, r_out, gate,
):
    tokens = q_ref.shape[0]
    groups = 4
    me_c, me_j = lax.axis_index("ctx"), lax.axis_index("head")
    half = ctx_count // 2
    flip = me_c // half
    group = lax.rem(me_j + 2 * flip, groups)
    sides = []
    for step in (ctx_count - 1, 1):
        c = lax.rem(me_c + step, ctx_count)
        sides.append((c, lax.rem(me_j + 2 * flip + 2 * (c // half), groups)))
    peers = [(r, lax.rem(me_j + r, groups), lax.rem(group + r, groups)) for r in (2, 1, 3)]
    my_rows = pl.ds(pl.multiple_of(me_j * tokens, tokens), tokens)

    def columns(which_group, head):
        return pl.ds(pl.multiple_of((which_group * heads + head) * HD, HD), HD)

    def remote(src, dst, send, recv, device):
        pltpu.make_async_remote_copy(
            src_ref=src, dst_ref=dst, send_sem=send, recv_sem=recv,
            device_id=device, device_id_type=MESH,
        ).start()

    def wait_bytes(ref, sem):
        pltpu.make_async_copy(ref, ref, sem).wait()

    loads = [
        pltpu.make_async_copy(src, dst, s_load.at[n])
        for n, (src, dst) in enumerate((
            (o_ref, o_buf), (do_ref, do_buf), (lse_hbm, lse_ref), (wm_hbm, wm_ref), (cf_hbm, cf_ref),
        ))
    ]
    for load in loads:
        load.start()

    leader = groups - 1
    barrier = pltpu.get_barrier_semaphore()
    for _, peer, peer_group in peers:
        @pl.when(peer_group != leader)
        def _():
            pl.semaphore_signal(barrier, inc=1, device_id=(me_c, peer), device_id_type=MESH)

    for c, _ in sides:
        side_leader = lax.rem(leader + 2 * (c // half), groups)
        pl.semaphore_signal(barrier, inc=1, device_id=(c, side_leader), device_id_type=MESH)

    @pl.when(group != leader)
    def _():
        pl.semaphore_wait(barrier, len(peers))

    for _, peer, peer_group in peers:
        @pl.when(peer_group == leader)
        def _():
            pl.semaphore_signal(gate, inc=1, device_id=(me_c, peer), device_id_type=MESH)

    @pl.when(group == leader)
    def _():
        pl.semaphore_wait(gate, len(peers))

    def meet_sides():
        @pl.when(group == leader)
        def _():
            pl.semaphore_wait(barrier, len(sides) * groups)
            for _, peer, _ in peers:
                pl.semaphore_signal(gate, inc=1, device_id=(me_c, peer), device_id_type=MESH)

        @pl.when(group != leader)
        def _():
            pl.semaphore_wait(gate, 1)

    def send_in(head, first, refs, sem):
        for index, ref in enumerate(refs):
            for _, peer, peer_group in peers:
                remote(
                    ref.at[:, columns(peer_group, head)],
                    own.at[head, first + index, my_rows],
                    s_in.at[head], sem.at[head], (me_c, peer),
                )
            pltpu.make_async_copy(
                ref.at[:, columns(group, head)],
                own.at[head, first + index, my_rows],
                sem.at[head],
            ).start()

    def send_queries(head):
        send_in(head, 0, (q_ref, do_ref), r_q)

    def send_keys(head):
        send_in(head, 2, (k_ref, v_ref), r_kv)

    send_queries(0)

    partner_rows = pl.ds(pl.multiple_of((1 - me_j // 2) * TILE, TILE), TILE)

    def send_halo_direct(head):
        for index, ref in enumerate((q_ref, do_ref)):
            for core in range(2):
                their_group = group + core * (1 - 2 * lax.rem(group, 2))
                for side, (c, j) in enumerate(sides):
                    remote(
                        ref.at[:, columns(their_group, head)],
                        halo.at[head, 1 - side, index, my_rows],
                        s_halo.at[head], r_halo.at[head, 1 - side],
                        (c, j + core * (1 - 2 * lax.rem(j, 2))),
                    )

    def send_halo(head):
        wait_bytes(own.at[head, 0:2], r_q.at[head])
        for side in range(2):
            remote(
                own.at[head, 0:2, partner_rows], halo.at[head, 1 - side, :, partner_rows],
                s_halo.at[head], r_halo.at[head, 1 - side], sides[side],
            )

    all_heads = groups * heads
    lane = lax.broadcasted_iota(jnp.int32, (tokens, HD), 1)

    def add_deltas(columns_f, first, last):
        for n in range(first, last):
            span = slice(n * HD, (n + 1) * HD)
            product = do_buf[:, span].astype(jnp.float32) * o_buf[:, span].astype(jnp.float32)
            columns_f = jnp.where(lane == n, jnp.sum(product, axis=1, keepdims=True), columns_f)
        return columns_f

    for load in loads:
        load.wait()
    rows[...] = add_deltas(jnp.zeros((tokens, HD), jnp.float32), 0, FIRST_DELTAS)
    send_keys(0)
    meet_sides()
    send_halo_direct(0)
    send_halo(0)
    send_queries(1)
    send_halo_direct(1)
    send_halo_direct(2)
    turned = add_deltas(rows[...], FIRST_DELTAS, all_heads).T
    for g in range(groups):
        stat_send[g] = jnp.zeros((16, tokens), jnp.float32)
        stat_send[g, 0:heads] = lse_ref[g * heads:(g + 1) * heads] * LOG2E
        stat_send[g, 8:8 + heads] = turned[g * heads:(g + 1) * heads]
    stat[me_j] = stat_send[group]
    for _, peer, peer_group in peers:
        remote(stat_send.at[peer_group], stat.at[me_j], s_stat, r_stat, (me_c, peer))
    send_queries(2)
    send_halo(1)
    send_keys(1)
    send_queries(3)
    wait_bytes(stat.at[0:3], r_stat)
    for side in range(2):
        remote(stat, stat_halo.at[1 - side], s_hstat, r_hstat.at[1 - side], sides[side])

    tiles = 2 * ctx_count

    def tile_at(shift):
        return lax.rem(2 * me_c + shift + tiles, tiles)

    def off_amount(shift_q, shift_k):
        e = shift_k - shift_q + WIN
        s, u = tile_at(shift_q), tile_at(shift_k)
        open_ctx = (cf_ref[s] == 0) | (cf_ref[u] == 1)
        ok = open_ctx if e == WIN else open_ctx & (wm_ref[e, s] == 1)
        return jnp.where(ok, jnp.float32(0.0), jnp.float32(OFF))

    off = {
        (s, u): off_amount(s, u) for s in range(-2, 4) for u in (0, 1) if abs(s - u) <= WIN
    }

    scale = HD ** -0.5

    def stat_row(ref_at, tile, row):
        return jnp.concatenate(
            [ref_at(2 * tile, row), ref_at(2 * tile + 1, row)], axis=1
        )

    def pair(k, v, kt, q, do, lse, delta):
        probs = jnp.exp2(
            lax.dot_general(k, q, NT, preferred_element_type=jnp.float32) * (scale * LOG2E) - lse
        )
        dprobs = lax.dot_general(v, do, NT, preferred_element_type=jnp.float32)
        dscores = (probs * (dprobs - delta)).astype(jnp.bfloat16)
        return (
            matmul(dscores, q),
            matmul(probs.astype(jnp.bfloat16), do),
            matmul(kt, dscores),
        )

    def load_keys(head):
        made = []
        for t in range(2):
            span = pl.ds(t * TILE, TILE)
            k = own[head, 2, span]
            made.append((k, own[head, 3, span], k.T))
        return made

    def own_pairs(head):
        keys = load_keys(head)
        for s in range(2):
            span = pl.ds(s * TILE, TILE)
            q, do = own[head, 0, span], own[head, 1, span]
            row = lambda b, r: stat[b, pl.ds(r, 1)]
            lse, delta = stat_row(row, s, head), stat_row(row, s, head + 8)
            dq = None
            for t in range(2):
                dk, dv, term = pair(*keys[t], q, do, lse + off[s, t], delta)
                acc_kv[0, t] += dk
                acc_kv[1, t] += dv
                dq = term if dq is None else dq + term
            acc_q[head, s] = dq
        for t in range(2):
            span = pl.ds(t * TILE, TILE)
            out[head, 1, span] = (acc_kv[0, t] * scale).astype(jnp.bfloat16)
            out[head, 2, span] = acc_kv[1, t].astype(jnp.bfloat16)

    def halo_pairs(head):
        keys = load_keys(head)
        for side in (1, 0):
            for s in range(2):
                shift = s - 2 if side == 0 else s + 2
                span = pl.ds(s * TILE, TILE)
                q, do = halo[head, side, 0, span], halo[head, side, 1, span]
                row = lambda b, r: stat_halo[side, b, pl.ds(r, 1)]
                lse, delta = stat_row(row, s, head), stat_row(row, s, head + 8)
                dq = None
                for t in range(2):
                    if (shift, t) not in off:
                        continue
                    dk, dv, term = pair(*keys[t], q, do, lse + off[shift, t], delta)
                    if (side, s) == (1, 0):
                        acc_kv[0, t], acc_kv[1, t] = dk, dv
                    else:
                        acc_kv[0, t] += dk
                        acc_kv[1, t] += dv
                    dq = term if dq is None else dq + term
                part_send[head, side, s] = (dq * scale).astype(jnp.bfloat16)
                remote(
                    part_send.at[head, side, s], part.at[head, 1 - side, s],
                    s_part.at[head], r_part.at[head, s], sides[side],
                )

    outputs = (dq_ref, dk_ref, dv_ref)

    def send_out(head, which):
        for index in which:
            target = outputs[index].at[:, columns(group, head)]
            for _, peer, _ in peers:
                rows_there = pl.ds(pl.multiple_of(peer * tokens, tokens), tokens)
                remote(
                    out.at[head, index, rows_there], target,
                    s_out.at[head], r_out.at[index], (me_c, peer),
                )
            pltpu.make_async_copy(out.at[head, index, my_rows], target, r_out.at[index]).start()

    def finish_q(head):
        for s in range(2):
            wait_bytes(part.at[head, :, s], r_part.at[head, s])
            total = acc_q[head, s] * scale
            total = total + part[head, 0, s].astype(jnp.float32)
            total = total + part[head, 1, s].astype(jnp.float32)
            out[head, 0, pl.ds(s * TILE, TILE)] = total.T.astype(jnp.bfloat16)
            target = outputs[0].at[:, columns(group, head)]
            for peer in (2 * s, 2 * s + 1):
                source = out.at[head, 0, pl.ds(peer * tokens, tokens)]

                @pl.when(peer != me_j)
                def _():
                    remote(source, target, s_out.at[head], r_out.at[0], (me_c, peer))

                @pl.when(peer == me_j)
                def _():
                    pltpu.make_async_copy(source, target, r_out.at[0]).start()

    def step(i, carry):
        @pl.when(i + 1 < heads)
        def _():
            send_halo(i + 1)
            send_keys(i + 1)

        @pl.when(i + 2 < heads)
        def _():
            send_halo_direct(i + 2)

        @pl.when(i + 3 < heads)
        def _():
            send_queries(i + 3)

        @pl.when(i == 1)
        def _():
            for side in range(2):
                wait_bytes(stat_halo.at[side], r_hstat.at[side])

        @pl.when(i <= heads)
        def _():
            head = i - 1
            wait_bytes(own.at[head, 2:4], r_kv.at[head])
            for side in range(2):
                wait_bytes(halo.at[head, side], r_halo.at[head, side])
            halo_pairs(head)
            own_pairs(head)
            send_out(head, (1, 2))

        @pl.when(i >= 3)
        def _():
            head = i - 3
            finish_q(head)

        return carry

    lax.fori_loop(1, heads + 3, step, 0)

    wait_bytes(stat.at[0:3], s_stat)
    wait_bytes(stat_halo, s_hstat)

    def drain(head, carry):
        wait_bytes(own.at[head, :, pl.ds(0, 3 * tokens)], s_in.at[head])
        wait_bytes(own.at[head], s_halo.at[head])
        wait_bytes(part_send.at[head], s_part.at[head])
        wait_bytes(out.at[head, :, pl.ds(0, 3 * tokens)], s_out.at[head])
        return carry

    lax.fori_loop(0, heads, drain, 0)
    for index in range(3):
        wait_bytes(outputs[index], r_out.at[index])


def copy_out(*refs):
    sems = refs[6]
    copies = [pltpu.make_async_copy(refs[n], refs[3 + n], sems.at[n]) for n in range(3)]
    for copy in copies:
        copy.start()
    for copy in copies:
        copy.wait()


def per_device(queries, keys, values, outputs, out_grads, log_sums, window_mask, context_flag):
    tokens, width = queries.shape
    ctx_count, groups = lax.axis_size("ctx"), lax.axis_size("head")
    heads = log_sums.shape[1] // groups
    block = groups * tokens
    bf16, f32 = jnp.bfloat16, jnp.float32
    dma, vmem = pltpu.SemaphoreType.DMA, pltpu.VMEM
    anywhere = pl.BlockSpec(memory_space=pl.ANY)
    grads = pl.pallas_call(
        functools.partial(kernel, ctx_count, heads),
        out_shape=[vmem((tokens, width), bf16)] * 3,
        in_specs=[anywhere] * 8,
        out_specs=[anywhere] * 3,
        scratch_shapes=[
            vmem((heads, 4, block, HD), bf16),
            vmem((heads, 2, 2, block, HD), bf16),
            vmem((groups, 16, tokens), f32),
            vmem((groups, 16, tokens), f32),
            vmem((2, groups, 16, tokens), f32),
            vmem((tokens, width), bf16),
            vmem((tokens, width), bf16),
            vmem(log_sums.shape[::-1], f32),
            pltpu.SMEM(window_mask.shape[::-1], jnp.int32),
            pltpu.SMEM(context_flag.shape, jnp.int32),
            vmem((tokens, HD), f32),
            vmem((2, 2, TILE, HD), f32),
            vmem((heads, 2, HD, TILE), f32),
            vmem((heads, 2, 2, HD, TILE), bf16),
            vmem((heads, 2, 2, HD, TILE), bf16),
            vmem((heads, 3, block, HD), bf16),
            dma((5,)),
            dma((heads,)),
            dma((heads,)),
            dma((heads,)),
            dma,
            dma,
            dma,
            dma((2,)),
            dma((heads,)),
            dma((heads, 2)),
            dma((heads,)),
            dma((heads, 2)),
            dma((heads,)),
            dma((3,)),
            pltpu.SemaphoreType.REGULAR,
        ],
        compiler_params=pltpu.CompilerParams(
            collective_id=0, has_side_effects=True, vmem_limit_bytes=60 * 1024 * 1024
        ),
        name="attention_grads",
    )(queries, keys, values, outputs, out_grads, log_sums.T, window_mask.T, context_flag)
    return pl.pallas_call(
        copy_out,
        out_shape=[jax.ShapeDtypeStruct((tokens, width), bf16)] * 3,
        in_specs=[pl.BlockSpec(memory_space=pltpu.VMEM)] * 3,
        out_specs=[anywhere] * 3,
        scratch_shapes=[dma((3,))],
        compiler_params=pltpu.CompilerParams(vmem_limit_bytes=8 * 1024 * 1024),
        name="results_out",
    )(*grads)


def solution(mesh):
    placed = (P(("ctx", "head"), None),) * 6 + (P(), P())
    return jax.shard_map(
        per_device,
        mesh=mesh,
        in_specs=placed,
        out_specs=(P(("ctx", "head"), None),) * 3,
        check_vma=False,
    )
```
